32 devices in a mesh: group: 2 (over x), dp: 2 (over core), tensor: 8 (over z, y).
Axes of the slice: x: 2, y: 2, z: 4, core: 2. Of those that a mesh axis runs over, the one named last changes fastest.
Arguments:
- hidden: bfloat16 [1024, 8192], P(('group', 'dp'), 'tensor'), parts along dimension 0, may hold values from -6 to 6
- norm_gain: float32 [2, 8192], replicated, may hold values from 0.1 to 1.9
- w_query: bfloat16 [2, 8192, 4096], P(None, None, 'tensor'), may hold values from -0.0625 to 0.0625
- w_kv: bfloat16 [2, 8192, 1024], P(None, None, 'tensor'), may hold values from -0.0625 to 0.0625
- w_out: bfloat16 [2, 4096, 8192], P(None, 'tensor'), may hold values from -0.125 to 0.125
- cache: bfloat16 [2, 1024, 64, 1024], P(None, ('group', 'dp', 'tensor')), parts along dimension 1, may hold values from -1000 to 1000
- lengths: int32 [1024], P(('group', 'dp')), parts along dimension 0, may hold values from 1 to 64, as said below
- exits: int32 [1024], P(('group', 'dp')), parts along dimension 0, may hold values from 1 to 2, as said below
Outputs:
- result: bfloat16 [1024, 8192], P(('group', 'dp'), 'tensor'), parts along dimension 0
The draws below stay inside these ranges and needn't reach their ends.
There are 2 independent parts, one for each index of `group`. The reference program is written for one: setup_inputs(seed, part) draws one part's arguments, and reference() takes and returns one part's arrays. A program takes and returns all parts, laid end to end along the dimension named above; an argument that names none is the same for every part. Nothing has to cross between parts.
Inputs may be any that keep to these rules, and one draw needn't show every extreme that they name: `exits`: A row passes both layers where 2. Group the rows of every index of dp by place q // 32; over all indices of dp, exactly 32 rows of each such group pass both. How many of them stand on each index of dp varies. `lengths`: the new token stands at this position.
All inputs are finite; a program needn't handle non-finite values.
Results may differ from the reference program's by a relative error of at most 0.023.
Values may be sent and summed in bfloat16 or wider, within the bound.
No kernel may reach another device: no remote copies, remote signals or barrier semaphores. Data moves between devices by JAX's collectives and lax.ppermute only.
A program may use at most 192 MiB of HBM per device.

```python
import jax
import jax.numpy as jnp
from jax import lax

D = 8192
QH = 32
KVH = 4
HEAD_DIM = 128
ROWS_DEV = 256
CACHE_LEN = 64
CAP = 128
ROWS = 512
HEADS_DEV = 4
N_DP = 2
N_TENSOR = 8


def draw_exits(key, part):
    key = jax.random.fold_in(key, 21)
    key_noise, key_bias = jax.random.split(key)
    block_rows = ROWS_DEV // N_TENSOR
    row = jnp.arange(ROWS)
    owner = row // ROWS_DEV
    column = row % ROWS_DEV // block_rows
    bias = jax.random.randint(key_bias, (N_DP,), 0, 1024)
    noise = jax.random.randint(key_noise, (ROWS,), 0, 4096)
    score = (noise + bias[owner]) * ROWS + row
    same = column[:, None] == column[None, :]
    rank = jnp.sum(same & (score[None, :] > score[:, None]), axis=1)
    active_rows = (rank < N_DP * CAP // N_TENSOR).astype(jnp.int32)
    return (1 + active_rows).astype(jnp.int32)


def draw_lengths(key, part):
    key = jax.random.fold_in(key, 7)
    key_len, key_top = jax.random.split(key)
    spans = jax.random.randint(key_len, (ROWS,), 1, CACHE_LEN + 1)
    longest = jax.random.randint(key_top, (), 0, ROWS)
    return jnp.where(jnp.arange(ROWS) == longest, CACHE_LEN, spans).astype(jnp.int32)


def draw_cache(key, part):
    key = jax.random.fold_in(key, 11)
    key_base = jax.random.fold_in(key, 0)
    shape = (2, ROWS, CACHE_LEN, KVH, 2, HEAD_DIM)
    values = jax.random.normal(key_base, shape, jnp.float32)
    return values.reshape(2, ROWS, CACHE_LEN, KVH * 2 * HEAD_DIM).astype(jnp.bfloat16)


def spiked(drawn, stream_key, source, target, blocks, factor):
    def block_of(dim):
        return (jnp.arange(drawn.shape[dim]) // (drawn.shape[dim] // blocks)).reshape((-1,) + (1,) * (drawn.ndim - 1 - dim))

    first = jax.random.permutation(stream_key, blocks)[block_of(target)]
    other_side = (block_of(target) + blocks // 2) % blocks
    return jnp.where((block_of(source) == first) | (block_of(source) == other_side), factor * drawn, drawn)


def shard_levels(key, extent, cuts, least, high):
    level, own = 1.0, jax.random.fold_in(key, 6)
    for axis_at, blocks in cuts:
        heights = jnp.exp(jax.random.uniform(jax.random.fold_in(own, axis_at), (blocks,), jnp.float32, least / len(cuts), high / len(cuts)))
        level = level * jnp.repeat(heights, extent[axis_at] // blocks).reshape([-1 if axis == axis_at else 1 for axis in range(len(extent))])
    return level


def centred(own_key, extent, spread, bound, cuts=(), kind=jnp.bfloat16):
    drawn = spread * jax.random.normal(own_key, extent, jnp.float32)
    if cuts:
        drawn = drawn * shard_levels(own_key, extent, cuts, -0.22, 0.18)
    return jnp.clip(drawn, -bound, bound).astype(kind)


def bell_draw_with(key, dims, width, reach, cuts, heavy, held_as=jnp.bfloat16):
    entries = width * jax.random.normal(key, dims, jnp.float32)
    if cuts:
        entries = entries * shard_levels(key, dims, cuts, -0.22, 0.18)
    return jnp.clip(spiked(entries, jax.random.fold_in(key, 3), *heavy), -reach, reach).astype(held_as)


def setup_inputs(seed: int = 0, part: int = 0) -> dict:
    streams_of = jax.random.split(jax.random.key(seed), 9)
    part_splits = jax.random.split(jax.random.fold_in(streams_of[8], part), 9)
    hidden = centred(part_splits[0], (ROWS, D), 1.0, 6.0, ((0, 2), (1, 8)))
    norm_gain = jnp.clip(1.0 + 0.18 * jax.random.normal(streams_of[1], (2, D), jnp.float32), 0.1, 1.9)
    w_query = centred(streams_of[2], (2, D, QH * HEAD_DIM), D ** -0.5, 0.0625, ((2, 8),))
    w_kv = centred(streams_of[3], (2, D, 2 * KVH * HEAD_DIM), D ** -0.5, 0.0625, ((2, 8),))
    w_out = bell_draw_with(streams_of[4], (2, QH * HEAD_DIM, D), (QH * HEAD_DIM) ** -0.5, 0.125, ((1, 8),), (1, 2, 8, 2.0))
    cache = draw_cache(jax.random.fold_in(jax.random.fold_in(streams_of[8], part), 71), part)
    lengths = draw_lengths(jax.random.fold_in(jax.random.fold_in(streams_of[8], part), 71), part)
    exits = draw_exits(jax.random.fold_in(jax.random.fold_in(streams_of[8], part), 71), part)
    return {"hidden": hidden, "norm_gain": norm_gain, "w_query": w_query, "w_kv": w_kv, "w_out": w_out, "cache": cache, "lengths": lengths, "exits": exits}


EPS = 1e-05
ROPE_BASE = 500000.0

def rotate(values, position):
    half = values.shape[-1] // 2
    freqs = ROPE_BASE ** (-jnp.arange(half, dtype=jnp.float32) / half)
    angle = position.astype(jnp.float32)[:, None] * freqs[None, :]
    cosine = jnp.cos(angle)[:, None, :]
    sine = jnp.sin(angle)[:, None, :]
    front = values[..., :half]
    back = values[..., half:]
    return jnp.concatenate([front * cosine - back * sine, back * cosine + front * sine], axis=-1)

def attention_layer(level, hidden, norm_gain, w_query, w_kv, w_out, cache, lengths):
    count = hidden.shape[0]
    state = hidden.astype(jnp.float32)
    factor = lax.rsqrt(lax.optimization_barrier(jnp.sum(state * state, axis=1, keepdims=True)) / D + EPS)
    scaled = (state * norm_gain[level][None, :]).astype(jnp.bfloat16)
    query = jnp.dot(scaled, w_query[level], preferred_element_type=jnp.float32) * factor
    query = rotate(query.reshape(count, QH, HEAD_DIM), lengths).astype(jnp.bfloat16)
    fresh = (jnp.dot(scaled, w_kv[level], preferred_element_type=jnp.float32) * factor).astype(jnp.bfloat16)
    new_keys = rotate(fresh[:, :KVH * HEAD_DIM].reshape(count, KVH, HEAD_DIM).astype(jnp.float32), lengths).astype(jnp.bfloat16)
    new_values = fresh[:, KVH * HEAD_DIM:].reshape(count, KVH, HEAD_DIM).astype(jnp.float32)
    stored_cache = cache[level].reshape(count, CACHE_LEN, KVH, 2, HEAD_DIM).astype(jnp.float32)
    keys = stored_cache[:, :, :, 0]
    values = stored_cache[:, :, :, 1]
    grouped = query.reshape(count, KVH, QH // KVH, HEAD_DIM).astype(jnp.float32)
    scale = HEAD_DIM ** (-0.5)
    scores = jnp.einsum('rkgd,rpkd->rkgp', grouped, keys) * scale
    own_score = jnp.einsum('rkgd,rkd->rkg', grouped, new_keys.astype(jnp.float32)) * scale
    valid = (jnp.arange(CACHE_LEN)[None, :] < lengths[:, None])[:, None, None, :]
    highest = jnp.maximum(lax.optimization_barrier(jnp.max(jnp.where(valid, scores, -1e+30), axis=-1)), own_score)
    weights = jnp.where(valid, jnp.exp(scores - highest[..., None]), 0.0)
    own_weight = jnp.exp(own_score - highest)
    total = lax.optimization_barrier(jnp.sum(weights, axis=-1)) + own_weight
    mixed = jnp.einsum('rkgp,rpkd->rkgd', weights, values) + own_weight[..., None] * new_values[:, :, None, :]
    attended = (mixed / total[..., None]).astype(jnp.bfloat16).reshape(count, QH * HEAD_DIM)
    block = HEADS_DEV * HEAD_DIM
    branch_part = jnp.zeros((count, D), jnp.float32)
    for shard in range(N_TENSOR):
        term = jnp.dot(attended[:, shard * block:(shard + 1) * block], w_out[level][shard * block:(shard + 1) * block], preferred_element_type=jnp.float32).astype(jnp.bfloat16)
        branch_part = branch_part + lax.optimization_barrier(term).astype(jnp.float32)
    return (state + branch_part).astype(jnp.bfloat16)

def reference(hidden, norm_gain, w_query, w_kv, w_out, cache, lengths, exits):
    first = attention_layer(0, hidden, norm_gain, w_query, w_kv, w_out, cache, lengths)
    second = attention_layer(1, first, norm_gain, w_query, w_kv, w_out, cache, lengths)
    return jnp.where(exits[:, None] == 2, second, first)
```

```python
import functools

import jax
import jax.numpy as jnp
from jax import lax
from jax.experimental import pallas as pl
from jax.experimental.pallas import tpu as pltpu
from jax.sharding import PartitionSpec as P

QH = 32
KVH = 4
HEAD_DIM = 128

EPS = 1e-05
ROPE_BASE = 500000.0
NEGATIVE = -1e30
VMEM_LIMIT = 40 * 1024 * 1024


def ring_order(mesh):
    count = mesh.shape["tensor"]
    natural = list(range(count))
    if count % 2 or count < 4:
        return natural
    axis = mesh.axis_names.index("tensor")
    places = [getattr(d, "coords", None) for d in jnp_line(mesh, axis)]
    if all(place is not None for place in places):
        steps = [sum(abs(a - b) for a, b in zip(p, q)) for p, q in zip(places, places[1:])]
        if max(steps) <= 1:
            return natural
    return natural[0::2] + natural[1::2][::-1]


def jnp_line(mesh, axis):
    devices = mesh.devices
    index = [0] * devices.ndim
    index[axis] = slice(None)
    return list(devices[tuple(index)])


def params():
    return pltpu.CompilerParams(vmem_limit_bytes=VMEM_LIMIT)


def whole(*shape):
    return pl.BlockSpec(shape, lambda *_: (0,) * len(shape))


def deal_kernel(block_rows, marks_ref, spans_ref, own_ref, other_ref, first_ref, second_ref, stay_ref, leave_ref, span_ref, source_ref):
    rows = own_ref.shape[0]
    half = block_rows // 2
    part = rows // 2
    marks = marks_ref[...]
    down = lax.broadcasted_iota(jnp.int32, (rows, rows), 0)
    across = lax.broadcasted_iota(jnp.int32, (rows, rows), 1)
    same = (down // block_rows) == (across // block_rows)
    before = same & (down < across)
    marks16 = marks.astype(jnp.bfloat16)
    ranks = jnp.dot(marks16, before.astype(jnp.bfloat16), preferred_element_type=jnp.float32)
    totals = jnp.dot(marks16, same.astype(jnp.bfloat16), preferred_element_type=jnp.float32)

    def listed(which):
        count = totals[which : which + 1]
        place = jnp.where(marks[which : which + 1] > 0.5, ranks[which : which + 1], count + ranks[which + 2 : which + 3])
        low = jnp.minimum(count, float(half))
        high = jnp.maximum(count, float(half))
        return place, low, (place >= low) & (place < high)

    place, low, goes = listed(0)
    other_place, other_low, comes = listed(1)
    group = (lax.broadcasted_iota(jnp.int32, (1, rows), 1) // block_rows).astype(jnp.float32) * float(half)

    def slot(position):
        return jnp.where(position < float(half), group + position, group + position + float(part - half))

    stays_at = jnp.where(goes, -1.0, slot(place))
    comes_to = jnp.where(comes, slot(low + other_place - other_low), -1.0)
    leaves_to = jnp.where(goes, slot(other_low + place - low), -1.0)
    slots = down.astype(jnp.float32)
    stay = slots == stays_at
    come = slots == comes_to
    leave = slots == leaves_to
    stay16 = stay.astype(jnp.bfloat16)
    come16 = come.astype(jnp.bfloat16)
    moved = jnp.dot(stay16, own_ref[...], preferred_element_type=jnp.float32) + jnp.dot(
        come16, other_ref[...], preferred_element_type=jnp.float32
    )
    moved = moved.astype(jnp.bfloat16)
    first_ref[...] = moved[:part]
    second_ref[...] = moved[part:]
    stay_ref[...] = stay16
    leave_ref[...] = leave.astype(jnp.bfloat16)
    spans = spans_ref[...]
    local = (across % block_rows).astype(jnp.float32)
    span_ref[...] = jnp.sum(jnp.where(stay, spans[0:1], 0.0) + jnp.where(come, spans[1:2], 0.0), axis=1, keepdims=True)
    source_ref[...] = jnp.sum(jnp.where(stay, local, 0.0) + jnp.where(come, local + float(block_rows), 0.0), axis=1, keepdims=True)


def deal(block_rows, marks, spans, own, other):
    rows, width = own.shape
    shapes = [
        ((rows // 2, width), jnp.bfloat16),
        ((rows // 2, width), jnp.bfloat16),
        ((rows, rows), jnp.bfloat16),
        ((rows, rows), jnp.bfloat16),
        ((rows, 1), jnp.float32),
        ((rows, 1), jnp.float32),
    ]
    return pl.pallas_call(
        functools.partial(deal_kernel, block_rows),
        out_shape=[jax.ShapeDtypeStruct(*s) for s in shapes],
        compiler_params=params(),
        name="deal",
    )(marks, spans, own, other)


def restore_kernel(stay_ref, leave_ref, first_ref, second_ref, other_first_ref, other_second_ref, out_ref):
    part = first_ref.shape[0]

    def back(chosen, values):
        return lax.dot_general(chosen, values, (((0,), (0,)), ((), ())), preferred_element_type=jnp.float32)

    stay = stay_ref[...]
    leave = leave_ref[...]
    total = back(stay[:part], first_ref[...]) + back(stay[part:], second_ref[...])
    total = total + back(leave[:part], other_first_ref[...]) + back(leave[part:], other_second_ref[...])
    out_ref[...] = total.astype(jnp.bfloat16)


def restore(stay, leave, first, second, other_first, other_second):
    return pl.pallas_call(
        restore_kernel,
        out_shape=jax.ShapeDtypeStruct((stay.shape[1], first.shape[1]), jnp.bfloat16),
        compiler_params=params(),
        name="restore",
    )(stay, leave, first, second, other_first, other_second)


def project_kernel(level, count, steps, width, has_sum, finish, table_ref, *refs):
    refs = list(refs)
    blocks = [refs[4 * i : 4 * i + 4] for i in range(count)]
    refs = refs[4 * count :]
    if has_sum:
        start, refs = refs[:3], refs[3:]
    if finish:
        cosine_ref, sine_ref, out_ref, query_ref, fresh_ref, square_ref = refs
    else:
        query_ref, fresh_ref, square_ref = refs
    step = pl.program_id(0)

    @pl.when(step == 0)
    def _():
        if has_sum:
            query_ref[...] = start[0][...]
            fresh_ref[...] = start[1][...]
            square_ref[...] = start[2][...]
        else:
            query_ref[...] = jnp.zeros_like(query_ref)
            fresh_ref[...] = jnp.zeros_like(fresh_ref)
            square_ref[...] = jnp.zeros_like(square_ref)

    query = query_ref[...]
    fresh = fresh_ref[...]
    square = square_ref[...]
    for value_ref, gain_ref, query_weight_ref, fresh_weight_ref in blocks:
        values = value_ref[...].astype(jnp.float32)
        scaled = (values * gain_ref[level : level + 1, :]).astype(jnp.bfloat16)
        query = query + jnp.dot(scaled, query_weight_ref[...], preferred_element_type=jnp.float32)
        fresh = fresh + jnp.dot(scaled, fresh_weight_ref[...], preferred_element_type=jnp.float32)
        squares = values * values
        for at in range(0, squares.shape[1], HEAD_DIM):
            square = square + squares[:, at : at + HEAD_DIM]
    query_ref[...] = query
    fresh_ref[...] = fresh
    square_ref[...] = square

    if finish:

        @pl.when(step == steps - 1)
        def _():
            factor = lax.rsqrt(jnp.sum(square, axis=1, keepdims=True) / width + EPS)
            cosine = cosine_ref[...]
            sine = sine_ref[...]
            columns = query.shape[1]
            for at in range(0, columns, HEAD_DIM):
                head = query[:, at : at + HEAD_DIM] * factor
                turned = head * cosine + pltpu.roll(head, HEAD_DIM // 2, 1) * sine
                out_ref[:, at : at + HEAD_DIM] = turned.astype(jnp.bfloat16)
            out_ref[:, columns:] = (fresh * factor).astype(jnp.bfloat16)


def project(level, table, gain, query_weight, fresh_weight, blocks, sums=None, rope=None):
    rows = blocks[0][0].shape[0]
    parts = table.shape[0]
    depth = query_weight.shape[1]
    tile = depth // parts // 2
    steps = blocks[0][0].shape[1] // tile
    columns = query_weight.shape[2]
    fresh_columns = fresh_weight.shape[2]
    in_specs = []
    operands = []
    for values, place, first in blocks:
        in_specs += [
            pl.BlockSpec((rows, tile), lambda k, t: (0, k)),
            pl.BlockSpec((2, tile), lambda k, t, place=place, first=first: (0, t[place] * 2 + first + k)),
            pl.BlockSpec((None, tile, columns), lambda k, t, place=place, first=first: (level, t[place] * 2 + first + k, 0)),
            pl.BlockSpec((None, tile, fresh_columns), lambda k, t, place=place, first=first: (level, t[place] * 2 + first + k, 0)),
        ]
        operands += [values, gain, query_weight, fresh_weight]
    sum_shapes = [(rows, columns), (rows, fresh_columns), (rows, HEAD_DIM)]
    if sums is not None:
        in_specs += [whole(*s) for s in sum_shapes]
        operands += list(sums)
    finish = rope is not None
    scratch = []
    if finish:
        in_specs += [whole(rows, HEAD_DIM)] * 2
        operands += list(rope)
        out_shape = jax.ShapeDtypeStruct((rows, columns + fresh_columns), jnp.bfloat16)
        out_specs = whole(rows, columns + fresh_columns)
        scratch = [pltpu.VMEM(s, jnp.float32) for s in sum_shapes]
    else:
        out_shape = [jax.ShapeDtypeStruct(s, jnp.float32) for s in sum_shapes]
        out_specs = [whole(*s) for s in sum_shapes]
    body = functools.partial(project_kernel, level, len(blocks), steps, depth, sums is not None, finish)
    flops = 2 * rows * tile * steps * len(blocks) * (columns + fresh_columns)
    return pl.pallas_call(
        body,
        out_shape=out_shape,
        grid_spec=pltpu.PrefetchScalarGridSpec(
            num_scalar_prefetch=1, grid=(steps,), in_specs=in_specs, out_specs=out_specs, scratch_shapes=scratch
        ),
        compiler_params=params(),
        cost_estimate=pl.CostEstimate(flops=flops, bytes_accessed=flops // rows, transcendentals=0),
        name="project",
    )(table, *operands)


def attend_kernel(level, block_rows, columns, source_ref, got_ref, cosine_ref, sine_ref, span_ref, own_ref, other_ref, out_ref, held, sems):
    parts, rows, _ = got_ref.shape
    slots = held.shape[1]
    copies = []
    for row in range(rows):
        source = source_ref[row]

        @pl.when(source < block_rows)
        def _():
            pltpu.make_async_copy(own_ref.at[level, source], held.at[row], sems.at[row]).start()

        @pl.when(source >= block_rows)
        def _():
            pltpu.make_async_copy(other_ref.at[level, source - block_rows], held.at[row], sems.at[row]).start()

    heads_dev = columns // HEAD_DIM
    group = QH // KVH
    fresh = jnp.concatenate([got_ref[s, :, columns:].astype(jnp.float32) for s in range(parts)], axis=1)
    cosine = cosine_ref[...]
    sine = sine_ref[...]
    scale = HEAD_DIM ** (-0.5)
    total_rows = group * rows
    down = lax.broadcasted_iota(jnp.int32, (total_rows, rows * slots), 0)
    across = lax.broadcasted_iota(jnp.int32, (total_rows, rows * slots), 1)
    valid = ((down % rows) == (across // slots)) & ((across % slots).astype(jnp.float32) < span_ref[...])
    for row in range(rows):
        pltpu.make_async_copy(own_ref.at[level, 0], held.at[row], sems.at[row]).wait()
    for j in range(KVH):
        tiles = []
        for head in range(j * group, (j + 1) * group):
            at = head % heads_dev * HEAD_DIM
            tiles.append(got_ref[head // heads_dev, :, at : at + HEAD_DIM].astype(jnp.float32))
        query = jnp.concatenate(tiles, axis=0)
        new_key = fresh[:, j * HEAD_DIM : (j + 1) * HEAD_DIM]
        new_key = new_key * cosine + pltpu.roll(new_key, HEAD_DIM // 2, 1) * sine
        new_key = new_key.astype(jnp.bfloat16).astype(jnp.float32)
        new_value = fresh[:, (KVH + j) * HEAD_DIM : (KVH + j + 1) * HEAD_DIM]
        keys = held[:, :, 2 * j * HEAD_DIM : (2 * j + 1) * HEAD_DIM].reshape(rows * slots, HEAD_DIM)
        values = held[:, :, (2 * j + 1) * HEAD_DIM : (2 * j + 2) * HEAD_DIM].reshape(rows * slots, HEAD_DIM)
        scores = lax.dot_general(
            query.astype(jnp.bfloat16), keys, (((1,), (1,)), ((), ())), preferred_element_type=jnp.float32
        )
        scores = jnp.where(valid, scores * scale, NEGATIVE)
        own = jnp.sum(query * jnp.concatenate([new_key] * group, axis=0), axis=1, keepdims=True) * scale
        highest = jnp.maximum(jnp.max(scores, axis=1, keepdims=True), own)
        weights = jnp.where(valid, jnp.exp(scores - highest), 0.0)
        own_weight = jnp.exp(own - highest)
        total = jnp.sum(weights, axis=1, keepdims=True) + own_weight
        mixed = jnp.dot(weights.astype(jnp.bfloat16), values, preferred_element_type=jnp.float32)
        mixed = (mixed + own_weight * jnp.concatenate([new_value] * group, axis=0)) / total
        for head in range(j * group, (j + 1) * group):
            at = head % heads_dev * HEAD_DIM
            tile = mixed[(head - j * group) * rows : (head - j * group + 1) * rows]
            out_ref[head // heads_dev, :, at : at + HEAD_DIM] = tile.astype(jnp.bfloat16)


def attend(level, got, columns, rope, span, source, own, other):
    parts, rows, _ = got.shape
    _, block_rows, slots, depth = own.shape
    return pl.pallas_call(
        functools.partial(attend_kernel, level, block_rows, columns),
        out_shape=jax.ShapeDtypeStruct((parts, rows, columns), jnp.bfloat16),
        in_specs=[
            pl.BlockSpec(memory_space=pltpu.SMEM),
            pl.BlockSpec(memory_space=pltpu.VMEM),
            pl.BlockSpec(memory_space=pltpu.VMEM),
            pl.BlockSpec(memory_space=pltpu.VMEM),
            pl.BlockSpec(memory_space=pltpu.VMEM),
            pl.BlockSpec(memory_space=pl.ANY),
            pl.BlockSpec(memory_space=pl.ANY),
        ],
        out_specs=pl.BlockSpec(memory_space=pltpu.VMEM),
        scratch_shapes=[pltpu.VMEM((rows, slots, depth), jnp.bfloat16), pltpu.SemaphoreType.DMA((rows,))],
        compiler_params=params(),
        cost_estimate=pl.CostEstimate(flops=10**8, bytes_accessed=rows * slots * depth * 2, transcendentals=0),
        name="attend",
    )(source, got, rope[0], rope[1], span, own, other)


def output_kernel(table_ref, value_ref, weight_ref, *out_refs):
    product = jnp.dot(value_ref[...], weight_ref[...], preferred_element_type=jnp.float32).astype(jnp.bfloat16)
    if len(out_refs) == 1:
        out_refs[0][...] = product
    else:
        width = product.shape[1] // 2
        out_refs[0][...] = product[:, :width]
        out_refs[1][...] = product[:, width:]


def output_blocks(level, table, values, weight, first, count):
    rows, depth = values.shape
    parts = table.shape[0]
    width = weight.shape[2] // parts
    if count == 1:
        out_shape = [jax.ShapeDtypeStruct((rows, width // 2), jnp.bfloat16)] * 2
        out_specs = [whole(rows, width // 2)] * 2
    else:
        out_shape = jax.ShapeDtypeStruct((count, rows, width), jnp.bfloat16)
        out_specs = pl.BlockSpec((None, rows, width), lambda k, t: (k, 0, 0))
    flops = 2 * rows * depth * width * count
    return pl.pallas_call(
        output_kernel,
        out_shape=out_shape,
        grid_spec=pltpu.PrefetchScalarGridSpec(
            num_scalar_prefetch=1,
            grid=(count,),
            in_specs=[
                whole(rows, depth),
                pl.BlockSpec((None, depth, width), lambda k, t: (level, 0, t[(first + k) % parts])),
            ],
            out_specs=out_specs,
        ),
        compiler_params=params(),
        cost_estimate=pl.CostEstimate(flops=flops, bytes_accessed=flops // rows, transcendentals=0),
        name="output",
    )(table, values, weight)


def layer(level, ring, table, share, rope, local_rope, span, source, own, other, gain, query_weight, fresh_weight, out_weight):
    parts = len(ring)
    half = parts // 2
    width = share.shape[1]
    rows = share.shape[0]
    forward = [(ring[i], ring[(i + 1) % parts]) for i in range(parts)]
    backward = [(ring[i], ring[(i - 1) % parts]) for i in range(parts)]

    def send(value, way):
        return lax.ppermute(value, "tensor", way)

    weights = (gain, query_weight, fresh_weight)
    sums = project(level, table, *weights, [(share, 0, 0)])
    ahead = behind = share
    for step in range(1, half):
        behind = send(behind, forward)
        ahead = send(ahead, backward)
        sums = project(level, table, *weights, [(behind, parts - step, 0), (ahead, step, 0)], sums)
    behind = send(behind[:, : width // 2], forward)
    ahead = send(ahead[:, width // 2 :], backward)
    mine = project(level, table, *weights, [(behind, half, 0), (ahead, half, 1)], sums, rope)

    columns = query_weight.shape[2]
    got = lax.all_to_all(
        mine.reshape(parts, rows // parts, mine.shape[1]), "tensor", split_axis=0, concat_axis=0, tiled=True
    )
    attended = attend(level, got, columns, local_rope, span, source, own, other)
    attended = lax.all_to_all(attended, "tensor", split_axis=0, concat_axis=0, tiled=True).reshape(rows, columns)

    to_front, to_back = output_blocks(level, table, attended, out_weight, half, 1)
    products = output_blocks(level, table, attended, out_weight, half + 1, parts - 1)

    def product(place):
        return products[(place - half - 1) % parts].astype(jnp.float32)

    from_back = send(to_front, forward).astype(jnp.float32)
    from_front = send(to_back, backward).astype(jnp.float32)
    for step in range(half - 1, 0, -1):
        to_front = product(step)
        to_back = product(-step)
        if step == half - 1:
            to_front = jnp.concatenate([to_front[:, : width // 2] + from_back, to_front[:, width // 2 :]], axis=1)
            to_back = jnp.concatenate([to_back[:, : width // 2], to_back[:, width // 2 :] + from_front], axis=1)
        else:
            to_front = to_front + from_back
            to_back = to_back + from_front
        from_back = send(to_front.astype(jnp.bfloat16), forward).astype(jnp.float32)
        from_front = send(to_back.astype(jnp.bfloat16), backward).astype(jnp.float32)
    total = product(0) + (from_back + from_front)
    return (share.astype(jnp.float32) + total).astype(jnp.bfloat16)


def local(ring, hidden, norm_gain, w_query, w_kv, w_out, cache, lengths, exits):
    parts = len(ring)
    rows, width = hidden.shape
    block_rows = rows // parts
    half = block_rows // 2
    part = rows // 2
    me = lax.axis_index("tensor")
    swap = [(0, 1), (1, 0)]
    places = [ring.index(i) for i in range(parts)]
    tables = jnp.array([[ring[(places[i] + r) % parts] for r in range(parts)] for i in range(parts)], jnp.int32)
    table = lax.dynamic_index_in_dim(tables, me, 0, False)

    facts = jnp.stack([exits, lengths])
    other_facts = lax.ppermute(facts, "dp", swap)
    other_hidden = lax.ppermute(hidden, "dp", swap)
    other_cache = lax.ppermute(cache, "dp", swap)
    marks = (jnp.stack([facts[0], other_facts[0]]) == 2).astype(jnp.float32)
    marks = jnp.concatenate([marks, 1.0 - marks, jnp.zeros((4, rows), jnp.float32)], axis=0)
    spans = jnp.stack([facts[1], other_facts[1]]).astype(jnp.float32)
    first, second, stay, leave, span, source = deal(block_rows, marks, spans, hidden, other_hidden)

    turns = HEAD_DIM // 2
    freqs = ROPE_BASE ** (-jnp.arange(turns, dtype=jnp.float32) / turns)
    angle = span * freqs[None, :]
    cosine = jnp.cos(angle)
    sine = jnp.sin(angle)
    cosine = jnp.concatenate([cosine, cosine], axis=1)
    sine = jnp.concatenate([-sine, sine], axis=1)
    slots = cache.shape[2]

    def facts_of(start):
        rope = (cosine[start : start + part], sine[start : start + part])
        at = start + me * half
        local_rope = tuple(lax.dynamic_slice_in_dim(v, at, half) for v in (cosine, sine))
        local_span = lax.dynamic_slice_in_dim(span, at, half)
        local_span = jnp.broadcast_to(local_span, (half, slots)).reshape(1, half * slots)
        local_source = lax.dynamic_slice_in_dim(source, at, half).reshape(half).astype(jnp.int32)
        return rope, local_rope, local_span, local_source, cache, other_cache

    weights = (norm_gain, w_query, w_kv, w_out)
    of_first = facts_of(0)
    of_second = facts_of(part)
    first = layer(0, ring, table, first, *of_first, *weights)
    second = layer(0, ring, table, second, *of_second, *weights)
    first = layer(1, ring, table, first, *of_first, *weights)
    other_second = lax.ppermute(second, "dp", swap)
    other_first = lax.ppermute(first, "dp", swap)
    return restore(stay, leave, first, second, other_first, other_second)


def solution(mesh):
    in_specs = (
        P(("group", "dp"), "tensor"),
        P(),
        P(None, None, "tensor"),
        P(None, None, "tensor"),
        P(None, "tensor", None),
        P(None, ("group", "dp", "tensor"), None, None),
        P(("group", "dp")),
        P(("group", "dp")),
    )
    out_specs = P(("group", "dp"), "tensor")
    body = functools.partial(local, ring_order(mesh))
    return jax.shard_map(body, mesh=mesh, in_specs=in_specs, out_specs=out_specs, check_vma=False)
```

```python
import functools

import jax
import jax.numpy as jnp
from jax import lax
from jax.experimental import pallas as pl
from jax.experimental.pallas import tpu as pltpu
from jax.sharding import PartitionSpec as P

QH = 32
KVH = 4
HEAD_DIM = 128

EPS = 1e-05
ROPE_BASE = 500000.0
NEGATIVE = -1e30
VMEM_LIMIT = 50 * 1024 * 1024
ATTEND_LIMIT = 57 * 1024 * 1024


def ring_order(mesh):
    count = mesh.shape["tensor"]
    natural = list(range(count))
    if count % 2 or count < 4:
        return natural
    axis = mesh.axis_names.index("tensor")
    places = [getattr(d, "coords", None) for d in jnp_line(mesh, axis)]
    if all(place is not None for place in places):
        steps = [sum(abs(a - b) for a, b in zip(p, q)) for p, q in zip(places, places[1:])]
        if max(steps) <= 1:
            return natural
    return natural[0::2] + natural[1::2][::-1]


def jnp_line(mesh, axis):
    devices = mesh.devices
    index = [0] * devices.ndim
    index[axis] = slice(None)
    return list(devices[tuple(index)])


def params(limit=None):
    return pltpu.CompilerParams(vmem_limit_bytes=limit or VMEM_LIMIT)


def after(value, *others):
    return lax.optimization_barrier((value, *others))[0]


IN_VMEM = pl.BlockSpec(memory_space=pltpu.VMEM)
IN_SMEM = pl.BlockSpec(memory_space=pltpu.SMEM)
IN_HBM = pl.BlockSpec(memory_space=pltpu.HBM)


def deal_kernel(block_rows, exits_ref, other_exits_ref, spans_ref, other_spans_ref, own_ref, other_ref, first_ref, second_ref, place_ref, span_ref, facts_ref):
    rows = own_ref.shape[0]
    half = block_rows // 2
    part = rows // 2
    own = (exits_ref[...] == 2).astype(jnp.float32)
    other = (other_exits_ref[...] == 2).astype(jnp.float32)
    line = lax.broadcasted_iota(jnp.int32, (8, rows), 0)
    marks = jnp.where(line == 0, own, jnp.where(line == 1, other, 0.0))
    marks = jnp.where(line == 2, 1.0 - own, jnp.where(line == 3, 1.0 - other, marks))
    down = lax.broadcasted_iota(jnp.int32, (rows, rows), 0)
    across = lax.broadcasted_iota(jnp.int32, (rows, rows), 1)
    same = (down // block_rows) == (across // block_rows)
    before = same & (down < across)
    marks16 = marks.astype(jnp.bfloat16)
    ranks = jnp.dot(marks16, before.astype(jnp.bfloat16), preferred_element_type=jnp.float32)
    totals = jnp.dot(marks16, same.astype(jnp.bfloat16), preferred_element_type=jnp.float32)

    def listed(which):
        count = totals[which : which + 1]
        place = jnp.where(marks[which : which + 1] > 0.5, ranks[which : which + 1], count + ranks[which + 2 : which + 3])
        low = jnp.minimum(count, float(half))
        high = jnp.maximum(count, float(half))
        return place, low, (place >= low) & (place < high)

    place, low, goes = listed(0)
    other_place, other_low, comes = listed(1)
    group = (lax.broadcasted_iota(jnp.int32, (1, rows), 1) // block_rows).astype(jnp.float32) * float(half)

    def slot(position):
        return jnp.where(position < float(half), group + position, group + position + float(part - half))

    stays_at = jnp.where(goes, -1.0, slot(place))
    comes_to = jnp.where(comes, slot(low + other_place - other_low), -1.0)
    leaves_to = jnp.where(goes, slot(other_low + place - low), -1.0)
    slots = down.astype(jnp.float32)
    stay = slots == stays_at
    come = slots == comes_to
    moved = jnp.dot(stay.astype(jnp.bfloat16), own_ref[...], preferred_element_type=jnp.float32) + jnp.dot(
        come.astype(jnp.bfloat16), other_ref[...], preferred_element_type=jnp.float32
    )
    moved = moved.astype(jnp.bfloat16)
    first_ref[...] = moved[:part]
    second_ref[...] = moved[part:]
    place_ref[0:1, :] = stays_at
    place_ref[1:2, :] = leaves_to
    spans = spans_ref[...].astype(jnp.float32)
    other_spans = other_spans_ref[...].astype(jnp.float32)
    span_ref[...] = jnp.sum(jnp.where(stay, spans, 0.0) + jnp.where(come, other_spans, 0.0), axis=1, keepdims=True)
    local = (lax.broadcasted_iota(jnp.int32, (1, rows), 1) % block_rows).astype(jnp.float32)

    def along(chosen, lengths, places):
        told = jnp.where(line == 0, lengths, jnp.where(line == 1, places, 0.0)).astype(jnp.bfloat16)
        return lax.dot_general(
            told, chosen.astype(jnp.bfloat16), (((1,), (1,)), ((), ())), preferred_element_type=jnp.float32
        )

    facts = along(stay, spans, local) + along(come, other_spans, local + float(block_rows))
    facts_ref[...] = facts[0:2].astype(jnp.int32)


def deal(block_rows, exits, other_exits, spans, other_spans, own, other):
    rows, width = own.shape
    shapes = [
        ((rows // 2, width), jnp.bfloat16),
        ((rows // 2, width), jnp.bfloat16),
        ((2, rows), jnp.float32),
        ((rows, 1), jnp.float32),
        ((2, rows), jnp.int32),
    ]
    lines = [v.reshape(1, rows) for v in (exits, other_exits, spans, other_spans)]
    return pl.pallas_call(
        functools.partial(deal_kernel, block_rows),
        out_shape=[jax.ShapeDtypeStruct(*s) for s in shapes],
        compiler_params=params(),
        name="deal",
    )(*lines, own, other)


def restore_kernel(place_ref, first_ref, second_ref, other_first_ref, other_second_ref, out_ref):
    part = first_ref.shape[0]
    rows = out_ref.shape[0]
    slots = lax.broadcasted_iota(jnp.int32, (rows, rows), 0).astype(jnp.float32)

    def back(chosen, values):
        return lax.dot_general(chosen, values, (((0,), (0,)), ((), ())), preferred_element_type=jnp.float32)

    stay = (slots == place_ref[0:1, :]).astype(jnp.bfloat16)
    leave = (slots == place_ref[1:2, :]).astype(jnp.bfloat16)
    total = back(stay[:part], first_ref[...]) + back(stay[part:], second_ref[...])
    total = total + back(leave[:part], other_first_ref[...]) + back(leave[part:], other_second_ref[...])
    out_ref[...] = total.astype(jnp.bfloat16)


def restore(places, first, second, other_first, other_second):
    return pl.pallas_call(
        restore_kernel,
        out_shape=jax.ShapeDtypeStruct((places.shape[1], first.shape[1]), jnp.bfloat16),
        compiler_params=params(),
        name="restore",
    )(places, first, second, other_first, other_second)


def project_kernel(level, kinds, depth, has_sum, finish, table_ref, *refs):
    refs = list(refs)
    parts = table_ref.shape[0]
    width = depth // parts
    blocks = []
    for pieces, place in kinds:
        blocks.append((refs[:pieces], place))
        refs = refs[pieces:]
    gain_ref, query_weight_ref, fresh_weight_ref = refs[:3]
    *refs, query_held, fresh_held, sems = refs[3:]
    rows = blocks[0][0][0].shape[0]
    copies = []
    for index, (_, place) in enumerate(blocks):
        at = pl.ds(pl.multiple_of(table_ref[place] * width, width), width)
        pair = (
            pltpu.make_async_copy(query_weight_ref.at[level, at, :], query_held.at[index], sems.at[index, 0]),
            pltpu.make_async_copy(fresh_weight_ref.at[level, at, :], fresh_held.at[index], sems.at[index, 1]),
        )
        for copy in pair:
            copy.start()
        copies.append(pair)
    if has_sum:
        query, fresh, square = (ref[...] for ref in refs[:3])
        refs = refs[3:]
    else:
        query = jnp.zeros((rows, query_weight_ref.shape[2]), jnp.float32)
        fresh = jnp.zeros((rows, fresh_weight_ref.shape[2]), jnp.float32)
        square = jnp.zeros((rows, HEAD_DIM), jnp.float32)
    for index, (value_refs, place) in enumerate(blocks):
        at = pl.multiple_of(table_ref[place] * width, width)
        for copy in copies[index]:
            copy.wait()
        row = 0
        for value_ref in value_refs:
            span = value_ref.shape[1]
            values = value_ref[...].astype(jnp.float32)
            scaled = (values * gain_ref[level : level + 1, pl.ds(at, span)]).astype(jnp.bfloat16)
            query = query + jnp.dot(scaled, query_held[index, row : row + span], preferred_element_type=jnp.float32)
            fresh = fresh + jnp.dot(scaled, fresh_held[index, row : row + span], preferred_element_type=jnp.float32)
            squares = values * values
            for column in range(0, span, HEAD_DIM):
                square = square + squares[:, column : column + HEAD_DIM]
            at = at + span
            row += span
    if not finish:
        refs[0][...] = query
        refs[1][...] = fresh
        refs[2][...] = square
        return
    cosine_ref, sine_ref, out_ref = refs
    factor = lax.rsqrt(jnp.sum(square, axis=1, keepdims=True) / depth + EPS)
    cosine = cosine_ref[...]
    sine = sine_ref[...]
    columns = query.shape[1]
    for column in range(0, columns, HEAD_DIM):
        head = query[:, column : column + HEAD_DIM] * factor
        turned = head * cosine + pltpu.roll(head, HEAD_DIM // 2, 1) * sine
        out_ref[:, column : column + HEAD_DIM] = turned.astype(jnp.bfloat16)
    out_ref[:, columns:] = (fresh * factor).astype(jnp.bfloat16)


def project(level, table, gain, query_weight, fresh_weight, blocks, sums=None, rope=None):
    rows = blocks[0][0][0].shape[0]
    parts = table.shape[0]
    depth = query_weight.shape[1]
    columns = query_weight.shape[2]
    fresh_columns = fresh_weight.shape[2]
    operands = [table]
    for values, _ in blocks:
        operands += list(values)
    operands += [gain, query_weight, fresh_weight]
    if sums is not None:
        operands += list(sums)
    if rope is not None:
        operands += list(rope)
        out_shape = jax.ShapeDtypeStruct((rows, columns + fresh_columns), jnp.bfloat16)
    else:
        out_shape = [jax.ShapeDtypeStruct((rows, n), jnp.float32) for n in (columns, fresh_columns, HEAD_DIM)]
    kinds = [(len(values), place) for values, place in blocks]
    body = functools.partial(project_kernel, level, kinds, depth, sums is not None, rope is not None)
    flops = 2 * rows * (depth // table.shape[0]) * len(blocks) * (columns + fresh_columns)
    return pl.pallas_call(
        body,
        out_shape=out_shape,
        in_specs=[IN_SMEM] + [IN_HBM if v is query_weight or v is fresh_weight else IN_VMEM for v in operands[1:]],
        out_specs=jax.tree.map(lambda _: IN_VMEM, out_shape),
        scratch_shapes=[
            pltpu.VMEM((len(blocks), depth // parts, columns), jnp.bfloat16),
            pltpu.VMEM((len(blocks), depth // parts, fresh_columns), jnp.bfloat16),
            pltpu.SemaphoreType.DMA((len(blocks), 2)),
        ],
        compiler_params=params(),
        cost_estimate=pl.CostEstimate(flops=flops, bytes_accessed=flops // rows, transcendentals=0),
        name="project",
    )(*operands)


def attend_kernel(level, start, columns, table_ref, facts_ref, got_ref, cosine_ref, sine_ref, own_ref, other_ref, out_ref, held, sems):
    parts, rows, _ = got_ref.shape
    block_rows = own_ref.shape[1]
    slots = held.shape[1]
    first = start + table_ref[0] * rows
    for row in range(rows):
        source = facts_ref[1, first + row]

        @pl.when(source < block_rows)
        def _():
            pltpu.make_async_copy(own_ref.at[level, source], held.at[row], sems.at[row]).start()

        @pl.when(source >= block_rows)
        def _():
            pltpu.make_async_copy(other_ref.at[level, source - block_rows], held.at[row], sems.at[row]).start()

    heads_dev = columns // HEAD_DIM
    group = QH // KVH
    fresh = jnp.concatenate([got_ref[s, :, columns:].astype(jnp.float32) for s in range(parts)], axis=1)
    mine = pl.ds(pl.multiple_of(first, rows), rows)
    cosine = cosine_ref[mine, :]
    sine = sine_ref[mine, :]
    scale = HEAD_DIM ** (-0.5)
    total_rows = group * rows
    across = lax.broadcasted_iota(jnp.int32, (1, rows * slots), 1)
    owner = across // slots
    span = jnp.zeros_like(across)
    for row in range(rows):
        span = jnp.where(owner == row, facts_ref[0, first + row], span)
    owner = jnp.where(across % slots < span, owner, -1)
    down = lax.broadcasted_iota(jnp.int32, (total_rows, 1), 0) % rows
    valid = down == owner
    for row in range(rows):
        pltpu.make_async_copy(own_ref.at[level, 0], held.at[row], sems.at[row]).wait()
    for j in range(KVH):
        tiles = []
        for head in range(j * group, (j + 1) * group):
            at = head % heads_dev * HEAD_DIM
            tiles.append(got_ref[head // heads_dev, :, at : at + HEAD_DIM].astype(jnp.float32))
        query = jnp.concatenate(tiles, axis=0)
        new_key = fresh[:, j * HEAD_DIM : (j + 1) * HEAD_DIM]
        new_key = new_key * cosine + pltpu.roll(new_key, HEAD_DIM // 2, 1) * sine
        new_key = new_key.astype(jnp.bfloat16).astype(jnp.float32)
        new_value = fresh[:, (KVH + j) * HEAD_DIM : (KVH + j + 1) * HEAD_DIM]
        keys = held[:, :, 2 * j * HEAD_DIM : (2 * j + 1) * HEAD_DIM].reshape(rows * slots, HEAD_DIM)
        values = held[:, :, (2 * j + 1) * HEAD_DIM : (2 * j + 2) * HEAD_DIM].reshape(rows * slots, HEAD_DIM)
        scores = lax.dot_general(
            query.astype(jnp.bfloat16), keys, (((1,), (1,)), ((), ())), preferred_element_type=jnp.float32
        )
        scores = jnp.where(valid, scores * scale, NEGATIVE)
        own = jnp.sum(query * jnp.concatenate([new_key] * group, axis=0), axis=1, keepdims=True) * scale
        highest = jnp.maximum(jnp.max(scores, axis=1, keepdims=True), own)
        weights = jnp.where(valid, jnp.exp(scores - highest), 0.0)
        own_weight = jnp.exp(own - highest)
        total = jnp.sum(weights, axis=1, keepdims=True) + own_weight
        mixed = jnp.dot(weights.astype(jnp.bfloat16), values, preferred_element_type=jnp.float32)
        mixed = (mixed + own_weight * jnp.concatenate([new_value] * group, axis=0)) / total
        for head in range(j * group, (j + 1) * group):
            at = head % heads_dev * HEAD_DIM
            tile = mixed[(head - j * group) * rows : (head - j * group + 1) * rows]
            out_ref[head // heads_dev, :, at : at + HEAD_DIM] = tile.astype(jnp.bfloat16)


def attend(level, start, table, got, columns, facts, cosine, sine, own, other):
    parts, rows, _ = got.shape
    _, _, slots, depth = own.shape
    return pl.pallas_call(
        functools.partial(attend_kernel, level, start, columns),
        out_shape=jax.ShapeDtypeStruct((parts, rows, columns), jnp.bfloat16),
        in_specs=[IN_SMEM, IN_SMEM, IN_VMEM, IN_VMEM, IN_VMEM, IN_HBM, IN_HBM],
        out_specs=IN_VMEM,
        scratch_shapes=[pltpu.VMEM((rows, slots, depth), jnp.bfloat16), pltpu.SemaphoreType.DMA((rows,))],
        compiler_params=params(ATTEND_LIMIT),
        cost_estimate=pl.CostEstimate(flops=10**8, bytes_accessed=rows * slots * depth * 2, transcendentals=0),
        name="attend",
    )(table, facts, got, cosine, sine, own, other)


def output_kernel(level, table_ref, value_ref, weight_ref, front_ref, back_ref, *refs):
    parts = table_ref.shape[0]
    width = weight_ref.shape[2] // parts
    *out_refs, held, sems = refs
    copies = []
    order = sorted(range(parts), key=lambda place: -abs(place - parts // 2))[::-1]
    for place in order:
        at = pl.ds(pl.multiple_of(table_ref[place] * width, width), width)
        copies.append(pltpu.make_async_copy(weight_ref.at[level, :, at], held.at[place], sems.at[place]))
        copies[-1].start()
    values = value_ref[...]
    for place, copy in zip(order, copies):
        copy.wait()
        product = jnp.dot(values, held[place], preferred_element_type=jnp.float32).astype(jnp.bfloat16)
        if place == parts // 2:
            front_ref[...] = product[:, : width // 2]
            back_ref[...] = product[:, width // 2 :]
        else:
            out_refs[place - (place > parts // 2)][...] = product


def output_blocks(level, table, values, weight):
    rows, depth = values.shape
    parts = table.shape[0]
    width = weight.shape[2] // parts
    shapes = [(rows, width // 2)] * 2 + [(rows, width)] * (parts - 1)
    flops = 2 * rows * depth * width * parts
    return pl.pallas_call(
        functools.partial(output_kernel, level),
        out_shape=[jax.ShapeDtypeStruct(s, jnp.bfloat16) for s in shapes],
        in_specs=[IN_SMEM, IN_VMEM, IN_HBM],
        out_specs=[IN_VMEM] * (parts + 1),
        scratch_shapes=[pltpu.VMEM((parts, depth, width), jnp.bfloat16), pltpu.SemaphoreType.DMA((parts,))],
        compiler_params=params(),
        cost_estimate=pl.CostEstimate(flops=flops, bytes_accessed=flops // rows, transcendentals=0),
        name="output",
    )(table, values, weight)


class Layer:
    def __init__(self, level, start, ring, table, share, told, weights):
        self.level, self.start, self.ring, self.table, self.share = level, start, ring, table, share
        self.facts, self.cosine, self.sine, self.own, self.other = told
        self.gain, self.query_weight, self.fresh_weight, self.out_weight = weights
        self.half = len(ring) // 2
        self.ahead = self.behind = share
        self.blocks = [((share,), 0)]
        self.sums = None

    def hop(self, to_front, to_back, held):
        parts = len(self.ring)
        forward = [(self.ring[i], self.ring[(i + 1) % parts]) for i in range(parts)]
        backward = [(self.ring[i], self.ring[(i - 1) % parts]) for i in range(parts)]
        to_front, to_back = lax.optimization_barrier((to_front, to_back, held))[:2]
        self.last = lax.ppermute(to_front, "tensor", forward), lax.ppermute(to_back, "tensor", backward)
        return self.last

    def gather(self, step, *held):
        width = self.share.shape[1] // 2
        if step < self.half:
            self.behind, self.ahead = self.hop(self.behind, self.ahead, held)
            self.blocks += [((self.behind,), -step % len(self.ring)), ((self.ahead,), step)]
        else:
            halves = self.hop(self.behind[:, :width], self.ahead[:, width:], held)
            self.blocks.append((halves, self.half))

    def project(self, places=None, final=False, held=()):
        weights = (self.gain, self.query_weight, self.fresh_weight)
        rope = None
        if final:
            rows = slice(self.start, self.start + self.share.shape[0])
            rope = self.cosine[rows], self.sine[rows]
        if places is None:
            blocks, self.blocks = self.blocks, []
        else:
            near = [min(place, len(self.ring) - place) <= places for _, place in self.blocks]
            blocks = [block for block, is_near in zip(self.blocks, near) if is_near]
            self.blocks = [block for block, is_near in zip(self.blocks, near) if not is_near]
        (values, place), *others = blocks
        values = (after(values[0], held), *values[1:])
        blocks = [(values, place), *others]
        self.sums = project(self.level, self.table, *weights, blocks, self.sums, rope)
        return self.sums

    def project_ring(self, steps, *held):
        first = 1 + sum(len(values) == 1 for values, _ in self.blocks) // 2
        for step in range(first, steps + 1):
            ready = self.sums if step > 2 else None
            self.gather(step, ready, *(held if step == first + 1 else ()))
            if 2 <= step < steps:
                self.project(step - 1)

    def ask(self, *held):
        parts = len(self.ring)
        mine = after(self.sums, held)
        mine = mine.reshape(parts, mine.shape[0] // parts, mine.shape[1])
        self.got = lax.all_to_all(mine, "tensor", split_axis=0, concat_axis=0, tiled=True)

    def attend(self, *held):
        columns = self.query_weight.shape[2]
        got = after(self.got, held)
        self.mixed = attend(
            self.level, self.start, self.table, got, columns, self.facts, self.cosine, self.sine, self.own, self.other
        )

    def answer(self, *held):
        mixed = after(self.mixed, held)
        back = lax.all_to_all(mixed, "tensor", split_axis=0, concat_axis=0, tiled=True)
        self.attended = back.reshape(self.share.shape[0], self.query_weight.shape[2])

    def output(self, *held):
        attended = after(self.attended, held)
        made = output_blocks(self.level, self.table, attended, self.out_weight)
        self.halves, self.products = made[:2], made[2:]

    def product(self, place):
        place = place % len(self.ring)
        return self.products[place - (place > self.half)].astype(jnp.float32)

    def scatter(self, step, *held):
        width = self.share.shape[1] // 2
        if step == 1:
            self.last = self.hop(*self.halves, held)
            return
        from_back, from_front = (v.astype(jnp.float32) for v in self.last)
        to_front = self.product(self.half + 1 - step)
        to_back = self.product(step - 1 - self.half)
        if step == 2:
            to_front = jnp.concatenate([to_front[:, :width] + from_back, to_front[:, width:]], axis=1)
            to_back = jnp.concatenate([to_back[:, :width], to_back[:, width:] + from_front], axis=1)
        else:
            to_front = to_front + from_back
            to_back = to_back + from_front
        self.hop(to_front.astype(jnp.bfloat16), to_back.astype(jnp.bfloat16), held)

    def result(self):
        from_back, from_front = (v.astype(jnp.float32) for v in self.last)
        total = self.product(0) + (from_back + from_front)
        return (self.share.astype(jnp.float32) + total).astype(jnp.bfloat16)


def local(ring, hidden, norm_gain, w_query, w_kv, w_out, cache, lengths, exits):
    parts = len(ring)
    rows, width = hidden.shape
    block_rows = rows // parts
    half = block_rows // 2
    part = rows // 2
    me = lax.axis_index("tensor")
    swap = [(0, 1), (1, 0)]
    places = [ring.index(i) for i in range(parts)]
    tables = jnp.array([[ring[(places[i] + r) % parts] for r in range(parts)] for i in range(parts)], jnp.int32)
    table = lax.dynamic_index_in_dim(tables, me, 0, False)

    other_exits = lax.ppermute(exits, "dp", swap)
    other_lengths = lax.ppermute(lengths, "dp", swap)
    other_hidden = lax.ppermute(hidden, "dp", swap)
    first, second, restored, span, facts = deal(
        block_rows, exits, other_exits, lengths, other_lengths, hidden, other_hidden
    )
    other_cache = lax.ppermute(after(cache, facts), "dp", swap)

    turns = HEAD_DIM // 2
    freqs = ROPE_BASE ** (-jnp.arange(turns, dtype=jnp.float32) / turns)
    angle = span * freqs[None, :]
    cosine = jnp.cos(angle)
    sine = jnp.sin(angle)
    cosine = jnp.concatenate([cosine, cosine], axis=1)
    sine = jnp.concatenate([-sine, sine], axis=1)

    told = facts, cosine, sine, cache, other_cache
    weights = (norm_gain, w_query, w_kv, w_out)
    steps = parts // 2
    a = Layer(0, 0, ring, table, first, told, weights)
    b = Layer(0, part, ring, table, second, told, weights)

    a.gather(1)
    a.project_ring(steps)
    b.gather(1, a.last)
    a.project(final=True)
    a.ask()
    for step in range(2, steps - 1):
        b.gather(step, a.sums)
    a.attend(b.last)
    a.answer()
    b.gather(steps - 1, a.got)
    b.project(2)
    a.output(b.last, b.sums)
    b.gather(steps, a.attended)
    a.scatter(1, b.last)
    a.scatter(2, a.products)
    b.project(final=True, held=a.products)
    for step in range(3, steps + 1):
        a.scatter(step, b.sums)
    b.ask()
    first = a.result()
    a = Layer(1, 0, ring, table, first, told, weights)
    a.gather(1, b.got)
    b.attend()
    b.answer()
    a.gather(2, b.mixed)
    b.output()
    a.project_ring(steps, b.products)
    b.scatter(1, a.last)
    a.project(final=True)
    a.ask()
    for step in range(2, steps - 1):
        b.scatter(step, a.sums)
    a.attend(b.last)
    a.answer()
    b.scatter(steps - 1, a.got)
    a.output(b.last)
    b.scatter(steps, a.attended)
    a.scatter(1, b.last)
    second = b.result()
    other_second = lax.ppermute(second, "dp", swap)
    for step in range(2, steps + 1):
        a.scatter(step)
    first = a.result()
    other_first = lax.ppermute(first, "dp", swap)
    return restore(restored, first, second, other_first, other_second)


def solution(mesh):
    in_specs = (
        P(("group", "dp"), "tensor"),
        P(),
        P(None, None, "tensor"),
        P(None, None, "tensor"),
        P(None, "tensor", None),
        P(None, ("group", "dp", "tensor"), None, None),
        P(("group", "dp")),
        P(("group", "dp")),
    )
    out_specs = P(("group", "dp"), "tensor")
    body = functools.partial(local, ring_order(mesh))
    return jax.shard_map(body, mesh=mesh, in_specs=in_specs, out_specs=out_specs, check_vma=False)
```

```python
import functools

import jax
import jax.numpy as jnp
from jax import lax
from jax.experimental import pallas as pl
from jax.experimental.pallas import tpu as pltpu
from jax.sharding import PartitionSpec as P

QH = 32
KVH = 4
HEAD_DIM = 128

EPS = 1e-05
ROPE_BASE = 500000.0
NEGATIVE = -1e30
VMEM_LIMIT = 50 * 1024 * 1024
ATTEND_LIMIT = 57 * 1024 * 1024
DEAL_LIMIT = 61 * 1024 * 1024


def ring_order(mesh):
    count = mesh.shape["tensor"]
    natural = list(range(count))
    if count % 2 or count < 4:
        return natural
    axis = mesh.axis_names.index("tensor")
    places = [getattr(d, "coords", None) for d in jnp_line(mesh, axis)]
    if all(place is not None for place in places):
        steps = [sum(abs(a - b) for a, b in zip(p, q)) for p, q in zip(places, places[1:])]
        if max(steps) <= 1:
            return natural
    return natural[0::2] + natural[1::2][::-1]


def jnp_line(mesh, axis):
    devices = mesh.devices
    index = [0] * devices.ndim
    index[axis] = slice(None)
    return list(devices[tuple(index)])


def params(limit=None):
    return pltpu.CompilerParams(vmem_limit_bytes=limit or VMEM_LIMIT)


def after(value, *others):
    return lax.optimization_barrier((value, *others))[0]


IN_VMEM = pl.BlockSpec(memory_space=pltpu.VMEM)
IN_SMEM = pl.BlockSpec(memory_space=pltpu.SMEM)
IN_HBM = pl.BlockSpec(memory_space=pltpu.HBM)


def deal_kernel(block_rows, exits_ref, other_exits_ref, spans_ref, other_spans_ref, own_ref, other_ref, first_ref, second_ref, place_ref, span_ref, facts_ref, *refs):
    *held, sems = refs
    rows = own_ref.shape[0]
    copies = []
    for index, ref in enumerate((exits_ref, other_exits_ref, spans_ref, other_spans_ref, own_ref, other_ref)):
        copies.append(pltpu.make_async_copy(ref, held[index], sems.at[index]))
        copies[-1].start()
    exits_ref, other_exits_ref, spans_ref, other_spans_ref, own_ref, other_ref = held
    for copy in copies[:4]:
        copy.wait()
    half = block_rows // 2
    part = rows // 2
    own = (exits_ref[...] == 2).astype(jnp.float32)
    other = (other_exits_ref[...] == 2).astype(jnp.float32)
    line = lax.broadcasted_iota(jnp.int32, (8, rows), 0)
    marks = jnp.where(line == 0, own, jnp.where(line == 1, other, 0.0))
    marks = jnp.where(line == 2, 1.0 - own, jnp.where(line == 3, 1.0 - other, marks))
    down = lax.broadcasted_iota(jnp.int32, (rows, rows), 0)
    across = lax.broadcasted_iota(jnp.int32, (rows, rows), 1)
    same = (down // block_rows) == (across // block_rows)
    before = same & (down < across)
    marks16 = marks.astype(jnp.bfloat16)
    ranks = jnp.dot(marks16, before.astype(jnp.bfloat16), preferred_element_type=jnp.float32)
    totals = jnp.dot(marks16, same.astype(jnp.bfloat16), preferred_element_type=jnp.float32)

    def listed(which):
        count = totals[which : which + 1]
        place = jnp.where(marks[which : which + 1] > 0.5, ranks[which : which + 1], count + ranks[which + 2 : which + 3])
        low = jnp.minimum(count, float(half))
        high = jnp.maximum(count, float(half))
        return place, low, (place >= low) & (place < high)

    place, low, goes = listed(0)
    other_place, other_low, comes = listed(1)
    group = (lax.broadcasted_iota(jnp.int32, (1, rows), 1) // block_rows).astype(jnp.float32) * float(half)

    def slot(position):
        return jnp.where(position < float(half), group + position, group + position + float(part - half))

    stays_at = jnp.where(goes, -1.0, slot(place))
    comes_to = jnp.where(comes, slot(low + other_place - other_low), -1.0)
    leaves_to = jnp.where(goes, slot(other_low + place - low), -1.0)
    slots = down.astype(jnp.float32)
    stay = slots == stays_at
    come = slots == comes_to
    for copy in copies[4:]:
        copy.wait()
    moved = jnp.dot(stay.astype(jnp.bfloat16), own_ref[...], preferred_element_type=jnp.float32) + jnp.dot(
        come.astype(jnp.bfloat16), other_ref[...], preferred_element_type=jnp.float32
    )
    moved = moved.astype(jnp.bfloat16)
    first_ref[...] = moved[:part]
    second_ref[...] = moved[part:]
    place_ref[0:1, :] = stays_at
    place_ref[1:2, :] = leaves_to
    spans = spans_ref[...].astype(jnp.float32)
    other_spans = other_spans_ref[...].astype(jnp.float32)
    span_ref[...] = jnp.sum(jnp.where(stay, spans, 0.0) + jnp.where(come, other_spans, 0.0), axis=1, keepdims=True)
    local = (lax.broadcasted_iota(jnp.int32, (1, rows), 1) % block_rows).astype(jnp.float32)

    def along(chosen, lengths, places):
        told = jnp.where(line == 0, lengths, jnp.where(line == 1, places, 0.0)).astype(jnp.bfloat16)
        return lax.dot_general(
            told, chosen.astype(jnp.bfloat16), (((1,), (1,)), ((), ())), preferred_element_type=jnp.float32
        )

    facts = along(stay, spans, local) + along(come, other_spans, local + float(block_rows))
    facts_ref[...] = facts[0:2].astype(jnp.int32)


def deal(block_rows, exits, other_exits, spans, other_spans, own, other):
    rows, width = own.shape
    shapes = [
        ((rows // 2, width), jnp.bfloat16),
        ((rows // 2, width), jnp.bfloat16),
        ((2, rows), jnp.float32),
        ((rows, 1), jnp.float32),
        ((2, rows), jnp.int32),
    ]
    lines = [v.reshape(1, rows) for v in (exits, other_exits, spans, other_spans)]
    return pl.pallas_call(
        functools.partial(deal_kernel, block_rows),
        out_shape=[jax.ShapeDtypeStruct(*s) for s in shapes],
        in_specs=[IN_HBM] * 6,
        out_specs=[IN_VMEM] * 5,
        scratch_shapes=[pltpu.VMEM(v.shape, v.dtype) for v in (*lines, own, other)] + [pltpu.SemaphoreType.DMA((6,))],
        compiler_params=params(DEAL_LIMIT),
        name="deal",
    )(*lines, own, other)


def restore_kernel(place_ref, first_ref, second_ref, other_first_ref, other_second_ref, out_ref):
    part = first_ref.shape[0]
    rows = out_ref.shape[0]
    slots = lax.broadcasted_iota(jnp.int32, (rows, rows), 0).astype(jnp.float32)

    def back(chosen, values):
        return lax.dot_general(chosen, values, (((0,), (0,)), ((), ())), preferred_element_type=jnp.float32)

    stay = (slots == place_ref[0:1, :]).astype(jnp.bfloat16)
    leave = (slots == place_ref[1:2, :]).astype(jnp.bfloat16)
    total = back(stay[:part], first_ref[...]) + back(stay[part:], second_ref[...])
    total = total + back(leave[:part], other_first_ref[...]) + back(leave[part:], other_second_ref[...])
    out_ref[...] = total.astype(jnp.bfloat16)


def restore(places, first, second, other_first, other_second):
    return pl.pallas_call(
        restore_kernel,
        out_shape=jax.ShapeDtypeStruct((places.shape[1], first.shape[1]), jnp.bfloat16),
        compiler_params=params(),
        name="restore",
    )(places, first, second, other_first, other_second)


def project_kernel(level, kinds, depth, has_sum, finish, table_ref, *refs):
    refs = list(refs)
    parts = table_ref.shape[0]
    width = depth // parts
    blocks = []
    for pieces, place in kinds:
        blocks.append((refs[:pieces], place))
        refs = refs[pieces:]
    gain_ref, query_weight_ref, fresh_weight_ref = refs[:3]
    *refs, query_held, fresh_held, sems = refs[3:]
    rows = blocks[0][0][0].shape[0]
    copies = []
    for index, (_, place) in enumerate(blocks):
        at = pl.ds(pl.multiple_of(table_ref[place] * width, width), width)
        pair = (
            pltpu.make_async_copy(query_weight_ref.at[level, at, :], query_held.at[index], sems.at[index, 0]),
            pltpu.make_async_copy(fresh_weight_ref.at[level, at, :], fresh_held.at[index], sems.at[index, 1]),
        )
        for copy in pair:
            copy.start()
        copies.append(pair)
    if has_sum:
        query, fresh, square = (ref[...] for ref in refs[:3])
        refs = refs[3:]
    else:
        query = jnp.zeros((rows, query_weight_ref.shape[2]), jnp.float32)
        fresh = jnp.zeros((rows, fresh_weight_ref.shape[2]), jnp.float32)
        square = jnp.zeros((rows, HEAD_DIM), jnp.float32)
    for index, (value_refs, place) in enumerate(blocks):
        at = pl.multiple_of(table_ref[place] * width, width)
        for copy in copies[index]:
            copy.wait()
        row = 0
        for value_ref in value_refs:
            span = value_ref.shape[1]
            values = value_ref[...].astype(jnp.float32)
            scaled = (values * gain_ref[level : level + 1, pl.ds(at, span)]).astype(jnp.bfloat16)
            query = query + jnp.dot(scaled, query_held[index, row : row + span], preferred_element_type=jnp.float32)
            fresh = fresh + jnp.dot(scaled, fresh_held[index, row : row + span], preferred_element_type=jnp.float32)
            squares = values * values
            for column in range(0, span, HEAD_DIM):
                square = square + squares[:, column : column + HEAD_DIM]
            at = at + span
            row += span
    if not finish:
        refs[0][...] = query
        refs[1][...] = fresh
        refs[2][...] = square
        return
    cosine_ref, sine_ref, out_ref = refs
    factor = lax.rsqrt(jnp.sum(square, axis=1, keepdims=True) / depth + EPS)
    cosine = cosine_ref[...]
    sine = sine_ref[...]
    columns = query.shape[1]
    for column in range(0, columns, HEAD_DIM):
        head = query[:, column : column + HEAD_DIM] * factor
        turned = head * cosine + pltpu.roll(head, HEAD_DIM // 2, 1) * sine
        out_ref[:, column : column + HEAD_DIM] = turned.astype(jnp.bfloat16)
    out_ref[:, columns:] = (fresh * factor).astype(jnp.bfloat16)


def project(level, table, gain, query_weight, fresh_weight, blocks, sums=None, rope=None):
    rows = blocks[0][0][0].shape[0]
    parts = table.shape[0]
    depth = query_weight.shape[1]
    columns = query_weight.shape[2]
    fresh_columns = fresh_weight.shape[2]
    operands = [table]
    for values, _ in blocks:
        operands += list(values)
    operands += [gain, query_weight, fresh_weight]
    if sums is not None:
        operands += list(sums)
    if rope is not None:
        operands += list(rope)
        out_shape = jax.ShapeDtypeStruct((rows, columns + fresh_columns), jnp.bfloat16)
    else:
        out_shape = [jax.ShapeDtypeStruct((rows, n), jnp.float32) for n in (columns, fresh_columns, HEAD_DIM)]
    kinds = [(len(values), place) for values, place in blocks]
    body = functools.partial(project_kernel, level, kinds, depth, sums is not None, rope is not None)
    flops = 2 * rows * (depth // table.shape[0]) * len(blocks) * (columns + fresh_columns)
    return pl.pallas_call(
        body,
        out_shape=out_shape,
        in_specs=[IN_SMEM] + [IN_HBM if v is query_weight or v is fresh_weight else IN_VMEM for v in operands[1:]],
        out_specs=jax.tree.map(lambda _: IN_VMEM, out_shape),
        scratch_shapes=[
            pltpu.VMEM((len(blocks), depth // parts, columns), jnp.bfloat16),
            pltpu.VMEM((len(blocks), depth // parts, fresh_columns), jnp.bfloat16),
            pltpu.SemaphoreType.DMA((len(blocks), 2)),
        ],
        compiler_params=params(),
        cost_estimate=pl.CostEstimate(flops=flops, bytes_accessed=flops // rows, transcendentals=0),
        name="project",
    )(*operands)


def attend_kernel(level, start, columns, table_ref, facts_ref, got_ref, cosine_ref, sine_ref, own_ref, other_ref, out_ref, held, sems):
    parts, rows, _ = got_ref.shape
    block_rows = own_ref.shape[1]
    slots = held.shape[1]
    first = start + table_ref[0] * rows
    for row in range(rows):
        source = facts_ref[1, first + row]

        @pl.when(source < block_rows)
        def _():
            pltpu.make_async_copy(own_ref.at[level, source], held.at[row], sems.at[row]).start()

        @pl.when(source >= block_rows)
        def _():
            pltpu.make_async_copy(other_ref.at[level, source - block_rows], held.at[row], sems.at[row]).start()

    heads_dev = columns // HEAD_DIM
    group = QH // KVH
    fresh = jnp.concatenate([got_ref[s, :, columns:].astype(jnp.float32) for s in range(parts)], axis=1)
    mine = pl.ds(pl.multiple_of(first, rows), rows)
    cosine = cosine_ref[mine, :]
    sine = sine_ref[mine, :]
    scale = HEAD_DIM ** (-0.5)
    total_rows = group * rows
    across = lax.broadcasted_iota(jnp.int32, (1, rows * slots), 1)
    owner = across // slots
    span = jnp.zeros_like(across)
    for row in range(rows):
        span = jnp.where(owner == row, facts_ref[0, first + row], span)
    owner = jnp.where(across % slots < span, owner, -1)
    down = lax.broadcasted_iota(jnp.int32, (total_rows, 1), 0) % rows
    valid = down == owner
    for row in range(rows):
        pltpu.make_async_copy(own_ref.at[level, 0], held.at[row], sems.at[row]).wait()
    for j in range(KVH):
        tiles = []
        for head in range(j * group, (j + 1) * group):
            at = head % heads_dev * HEAD_DIM
            tiles.append(got_ref[head // heads_dev, :, at : at + HEAD_DIM].astype(jnp.float32))
        query = jnp.concatenate(tiles, axis=0)
        new_key = fresh[:, j * HEAD_DIM : (j + 1) * HEAD_DIM]
        new_key = new_key * cosine + pltpu.roll(new_key, HEAD_DIM // 2, 1) * sine
        new_key = new_key.astype(jnp.bfloat16).astype(jnp.float32)
        new_value = fresh[:, (KVH + j) * HEAD_DIM : (KVH + j + 1) * HEAD_DIM]
        keys = held[:, :, 2 * j * HEAD_DIM : (2 * j + 1) * HEAD_DIM].reshape(rows * slots, HEAD_DIM)
        values = held[:, :, (2 * j + 1) * HEAD_DIM : (2 * j + 2) * HEAD_DIM].reshape(rows * slots, HEAD_DIM)
        scores = lax.dot_general(
            query.astype(jnp.bfloat16), keys, (((1,), (1,)), ((), ())), preferred_element_type=jnp.float32
        )
        scores = jnp.where(valid, scores * scale, NEGATIVE)
        own = jnp.sum(query * jnp.concatenate([new_key] * group, axis=0), axis=1, keepdims=True) * scale
        highest = jnp.maximum(jnp.max(scores, axis=1, keepdims=True), own)
        weights = jnp.exp(scores - highest)
        own_weight = jnp.exp(own - highest)
        total = jnp.sum(weights, axis=1, keepdims=True) + own_weight
        mixed = jnp.dot(weights.astype(jnp.bfloat16), values, preferred_element_type=jnp.float32)
        mixed = (mixed + own_weight * jnp.concatenate([new_value] * group, axis=0)) / total
        for head in range(j * group, (j + 1) * group):
            at = head % heads_dev * HEAD_DIM
            tile = mixed[(head - j * group) * rows : (head - j * group + 1) * rows]
            out_ref[head // heads_dev, :, at : at + HEAD_DIM] = tile.astype(jnp.bfloat16)


def attend(level, start, table, got, columns, facts, cosine, sine, own, other):
    parts, rows, _ = got.shape
    _, _, slots, depth = own.shape
    return pl.pallas_call(
        functools.partial(attend_kernel, level, start, columns),
        out_shape=jax.ShapeDtypeStruct((parts, rows, columns), jnp.bfloat16),
        in_specs=[IN_SMEM, IN_SMEM, IN_VMEM, IN_VMEM, IN_VMEM, IN_HBM, IN_HBM],
        out_specs=IN_VMEM,
        scratch_shapes=[pltpu.VMEM((rows, slots, depth), jnp.bfloat16), pltpu.SemaphoreType.DMA((rows,))],
        compiler_params=params(ATTEND_LIMIT),
        cost_estimate=pl.CostEstimate(flops=10**8, bytes_accessed=rows * slots * depth * 2, transcendentals=0),
        name="attend",
    )(table, facts, got, cosine, sine, own, other)


def output_kernel(level, table_ref, value_ref, weight_ref, front_ref, back_ref, *refs):
    parts = table_ref.shape[0]
    width = weight_ref.shape[2] // parts
    *out_refs, held, sems = refs
    copies = []
    order = sorted(range(parts), key=lambda place: -abs(place - parts // 2))[::-1]
    for place in order:
        at = pl.ds(pl.multiple_of(table_ref[place] * width, width), width)
        copies.append(pltpu.make_async_copy(weight_ref.at[level, :, at], held.at[place], sems.at[place]))
        copies[-1].start()
    values = value_ref[...]
    for place, copy in zip(order, copies):
        copy.wait()
        product = jnp.dot(values, held[place], preferred_element_type=jnp.float32).astype(jnp.bfloat16)
        if place == parts // 2:
            front_ref[...] = product[:, : width // 2]
            back_ref[...] = product[:, width // 2 :]
        else:
            out_refs[place - (place > parts // 2)][...] = product


def output_blocks(level, table, values, weight):
    rows, depth = values.shape
    parts = table.shape[0]
    width = weight.shape[2] // parts
    shapes = [(rows, width // 2)] * 2 + [(rows, width)] * (parts - 1)
    flops = 2 * rows * depth * width * parts
    return pl.pallas_call(
        functools.partial(output_kernel, level),
        out_shape=[jax.ShapeDtypeStruct(s, jnp.bfloat16) for s in shapes],
        in_specs=[IN_SMEM, IN_VMEM, IN_HBM],
        out_specs=[IN_VMEM] * (parts + 1),
        scratch_shapes=[pltpu.VMEM((parts, depth, width), jnp.bfloat16), pltpu.SemaphoreType.DMA((parts,))],
        compiler_params=params(),
        cost_estimate=pl.CostEstimate(flops=flops, bytes_accessed=flops // rows, transcendentals=0),
        name="output",
    )(table, values, weight)


class Layer:
    def __init__(self, level, start, ring, table, share, told, weights):
        self.level, self.start, self.ring, self.table, self.share = level, start, ring, table, share
        self.facts, self.cosine, self.sine, self.own, self.other = told
        self.gain, self.query_weight, self.fresh_weight, self.out_weight = weights
        self.half = len(ring) // 2
        self.ahead = self.behind = share
        self.blocks = [((share,), 0)]
        self.sums = None

    def hop(self, to_front, to_back, held, first):
        parts = len(self.ring)
        forward = [(self.ring[i], self.ring[(i + 1) % parts]) for i in range(parts)]
        backward = [(self.ring[i], self.ring[(i - 1) % parts]) for i in range(parts)]
        to_front, to_back = lax.optimization_barrier((to_front, to_back, held))[:2]
        self.last = lax.ppermute(to_front, "tensor", forward), lax.ppermute(to_back, "tensor", backward)
        if first:
            self.first_hop = self.last
        return self.last

    def gather(self, step, *held):
        width = self.share.shape[1] // 2
        if step < self.half:
            self.behind, self.ahead = self.hop(self.behind, self.ahead, held, step == 1)
            self.blocks += [((self.behind,), -step % len(self.ring)), ((self.ahead,), step)]
        else:
            halves = self.hop(self.behind[:, :width], self.ahead[:, width:], held, False)
            self.blocks.append((halves, self.half))

    def project(self, places=None, final=False, held=()):
        weights = (self.gain, self.query_weight, self.fresh_weight)
        rope = None
        if final:
            rows = slice(self.start, self.start + self.share.shape[0])
            rope = self.cosine[rows], self.sine[rows]
        if places is None:
            blocks, self.blocks = self.blocks, []
        else:
            near = [min(place, len(self.ring) - place) <= places for _, place in self.blocks]
            blocks = [block for block, is_near in zip(self.blocks, near) if is_near]
            self.blocks = [block for block, is_near in zip(self.blocks, near) if not is_near]
        (values, place), *others = blocks
        values = (after(values[0], held), *values[1:])
        blocks = [(values, place), *others]
        self.sums = project(self.level, self.table, *weights, blocks, self.sums, rope)
        return self.sums

    def project_ring(self, steps, *held):
        first = 1 + sum(len(values) == 1 for values, _ in self.blocks) // 2
        for step in range(first, steps + 1):
            ready = self.sums if step > 2 else None
            self.gather(step, ready, *(held if step == first + 1 else ()))
            if 2 <= step < steps:
                self.project(step - 1)

    def ask(self, *held):
        parts = len(self.ring)
        mine = after(self.sums, held)
        mine = mine.reshape(parts, mine.shape[0] // parts, mine.shape[1])
        self.got = lax.all_to_all(mine, "tensor", split_axis=0, concat_axis=0, tiled=True)

    def attend(self, *held):
        columns = self.query_weight.shape[2]
        got = after(self.got, held)
        self.mixed = attend(
            self.level, self.start, self.table, got, columns, self.facts, self.cosine, self.sine, self.own, self.other
        )

    def answer(self, *held):
        mixed = after(self.mixed, held)
        back = lax.all_to_all(mixed, "tensor", split_axis=0, concat_axis=0, tiled=True)
        self.attended = back.reshape(self.share.shape[0], self.query_weight.shape[2])

    def output(self, *held):
        attended = after(self.attended, held)
        made = output_blocks(self.level, self.table, attended, self.out_weight)
        self.halves, self.products = made[:2], made[2:]

    def product(self, place):
        place = place % len(self.ring)
        return self.products[place - (place > self.half)].astype(jnp.float32)

    def scatter(self, step, *held):
        width = self.share.shape[1] // 2
        if step == 1:
            self.hop(*self.halves, held, True)
            return
        from_back, from_front = (v.astype(jnp.float32) for v in self.last)
        to_front = self.product(self.half + 1 - step)
        to_back = self.product(step - 1 - self.half)
        if step == 2:
            to_front = jnp.concatenate([to_front[:, :width] + from_back, to_front[:, width:]], axis=1)
            to_back = jnp.concatenate([to_back[:, :width], to_back[:, width:] + from_front], axis=1)
        else:
            to_front = to_front + from_back
            to_back = to_back + from_front
        self.hop(to_front.astype(jnp.bfloat16), to_back.astype(jnp.bfloat16), held, False)

    def result(self):
        from_back, from_front = (v.astype(jnp.float32) for v in self.last)
        total = self.product(0) + (from_back + from_front)
        return (self.share.astype(jnp.float32) + total).astype(jnp.bfloat16)


def local(ring, hidden, norm_gain, w_query, w_kv, w_out, cache, lengths, exits):
    parts = len(ring)
    rows, width = hidden.shape
    block_rows = rows // parts
    half = block_rows // 2
    part = rows // 2
    me = lax.axis_index("tensor")
    swap = [(0, 1), (1, 0)]
    places = [ring.index(i) for i in range(parts)]
    tables = jnp.array([[ring[(places[i] + r) % parts] for r in range(parts)] for i in range(parts)], jnp.int32)
    table = lax.dynamic_index_in_dim(tables, me, 0, False)

    other_exits = lax.ppermute(exits, "dp", swap)
    other_lengths = lax.ppermute(lengths, "dp", swap)
    other_hidden = lax.ppermute(hidden, "dp", swap)
    first, second, restored, span, facts = deal(
        block_rows, exits, other_exits, lengths, other_lengths, hidden, other_hidden
    )
    other_cache = lax.ppermute(after(cache, facts), "dp", swap)

    turns = HEAD_DIM // 2
    freqs = ROPE_BASE ** (-jnp.arange(turns, dtype=jnp.float32) / turns)
    angle = span * freqs[None, :]
    cosine = jnp.cos(angle)
    sine = jnp.sin(angle)
    cosine = jnp.concatenate([cosine, cosine], axis=1)
    sine = jnp.concatenate([-sine, sine], axis=1)

    told = facts, cosine, sine, cache, other_cache
    weights = (norm_gain, w_query, w_kv, w_out)
    steps = parts // 2
    a = Layer(0, 0, ring, table, first, told, weights)
    b = Layer(0, part, ring, table, second, told, weights)

    a.gather(1)
    a.project_ring(steps, cosine, sine)
    a.project(steps - 1)
    b.gather(1, a.last, a.sums)
    a.project(final=True)
    a.ask()
    for step in range(2, steps - 1):
        b.gather(step, a.sums)
    a.attend(b.first_hop)
    b.gather(steps - 1, a.mixed)
    a.answer()
    b.gather(steps)
    a.output(b.last)
    a.scatter(1)
    b.project(steps - 2, held=a.products)
    a.scatter(2, b.sums)
    b.project(final=True)
    for step in range(3, steps + 1):
        a.scatter(step, b.sums)
    b.ask()
    first = a.result()
    a = Layer(1, 0, ring, table, first, told, weights)
    a.gather(1)
    b.attend(first)
    b.answer()
    a.gather(2, b.mixed)
    for step in range(3, steps):
        a.gather(step)
    b.output()
    a.project(steps - 2)
    a.gather(steps, b.products)
    b.scatter(1, a.last, a.sums)
    a.project(final=True)
    a.ask(b.last)
    for step in range(2, steps - 1):
        b.scatter(step, a.sums)
    a.attend()
    b.scatter(steps - 1, a.got)
    a.answer(b.last)
    b.scatter(steps, a.mixed)
    a.output(b.last)
    second = b.result()
    other_second = lax.ppermute(second, "dp", swap)
    for step in range(1, steps + 1):
        a.scatter(step)
    first = a.result()
    other_first = lax.ppermute(first, "dp", swap)
    return restore(restored, first, second, other_first, other_second)


def solution(mesh):
    in_specs = (
        P(("group", "dp"), "tensor"),
        P(),
        P(None, None, "tensor"),
        P(None, None, "tensor"),
        P(None, "tensor", None),
        P(None, ("group", "dp", "tensor"), None, None),
        P(("group", "dp")),
        P(("group", "dp")),
    )
    out_specs = P(("group", "dp"), "tensor")
    body = functools.partial(local, ring_order(mesh))
    return jax.shard_map(body, mesh=mesh, in_specs=in_specs, out_specs=out_specs, check_vma=False)
```
